32 devices in a mesh: group: 4 (over y, core), member: 8 (over z, x).
Axes of the slice: x: 2, y: 2, z: 4, core: 2. Of those that a mesh axis runs over, the one named last changes fastest.
Arguments:
- coefficients: float32 [256, 3, 289], P(('group', 'member')), may hold values from -2.5 to 2.5
- pair_list: int32 [512, 2], P(('group', 'member')), may hold values from -1 to 255, as said below
- pair_offset: float32 [512, 3], P(('group', 'member')), may hold values from -2.6 to 2.6
Outputs:
- force_coef: float32 [256, 3, 289], P(('group', 'member'))
The draws below stay inside these ranges and needn't reach their ends.
Inputs may be any that keep to these rules, and one draw needn't show every extreme that they name: `pair_list`: each row is (i, j) or (-1, -1) for an empty slot; on every device the live rows come first and some device has all 16 rows live. i is owned by a device of the pair owner's group; j is too, or else j is one of the first 4 vesicles of the device with the same member index in an adjacent group. Of one device's in-group entries (i and j), at most 4 are owned by any one device, and the full device reaches 4.
All inputs are finite; a program needn't handle non-finite values.
Results may differ from the reference program's by a relative error of at most 0.0003.
Values sent between devices are 32-bit elements; how exact they have to be, the bound alone decides.
A program may use at most 64 MiB of HBM per device.

```python
import math
import jax
import jax.numpy as jnp
from jax import lax

ORDER = 16
UPORDER = 32
NCOEF = 289
VES_DEV = 8
PAIR_DEV = 16
RIM_VES = 4
CAP = 4
VESICLES = 256
PAIRS = 512
N_GROUP = 4
N_MEMBER = 8
DEVICES = 32


def draw_coefficients(key, part):
    rough_key = jax.random.fold_in(key, 0)
    coef_index = jnp.arange(NCOEF)[None, :]
    component = jnp.arange(3)[:, None]
    sphere = math.sqrt(4.0 * math.pi / 3.0)
    sphere_part = jnp.where((component == 0) & (coef_index == 3), -sphere, 0.0)
    sphere_part = sphere_part + jnp.where((component == 1) & (coef_index == 1), -sphere, 0.0)
    sphere_part = sphere_part + jnp.where((component == 2) & (coef_index == 2), sphere, 0.0)
    rough_part = jnp.clip(jax.random.normal(rough_key, (VESICLES, 3, NCOEF), jnp.float32), -4.0, 4.0) * 0.06
    return (sphere_part[None, :, :].astype(jnp.float32) + rough_part).astype(jnp.float32)


def draw_pair_offset(key, part):
    height_key, turn_key, gap_key = jax.random.split(key, 3)
    height = jax.random.uniform(height_key, (PAIRS,), jnp.float32, -1.0, 1.0)
    turn = jax.random.uniform(turn_key, (PAIRS,), jnp.float32, -math.pi, math.pi)
    gap = jax.random.uniform(gap_key, (PAIRS,), jnp.float32, 0.05, 0.25)
    cycle = jnp.sqrt(jnp.maximum(1.0 - height * height, 0.0))
    reach = 2.0 + gap
    direction = jnp.stack([cycle * jnp.cos(turn), cycle * jnp.sin(turn), height], axis=-1)
    return (direction * reach[:, None]).astype(jnp.float32)


def draw_pair_list(key, part):
    key_list = jax.random.split(key, 8)
    device = jnp.arange(DEVICES)
    group_of = device // N_MEMBER
    member_of = device % N_MEMBER
    live_count = jax.random.randint(key_list[0], (DEVICES,), PAIR_DEV - PAIR_DEV // 4, PAIR_DEV + 1)
    full_device = jax.random.randint(key_list[1], (), 0, DEVICES)
    live_count = jnp.where(device == full_device, PAIR_DEV, live_count)
    owners_used = 2 * PAIR_DEV // CAP
    owner_order = jax.vmap(lambda sub_key: jax.random.permutation(sub_key, N_MEMBER))(jax.random.split(key_list[2], DEVICES))
    end_order = jax.vmap(lambda sub_key: jax.random.permutation(sub_key, 2 * PAIR_DEV))(jax.random.split(key_list[3], DEVICES))
    owner_pick = end_order % owners_used
    owner_member = jnp.take_along_axis(owner_order, owner_pick, axis=1)
    local_pick = jax.random.randint(key_list[4], (DEVICES, 2 * PAIR_DEV), 0, VES_DEV)
    inside_id = (group_of[:, None] * N_MEMBER + owner_member) * VES_DEV + local_pick
    ghost_flag = (jax.random.randint(key_list[5], (DEVICES, PAIR_DEV), 0, 16) == 0) & (owner_pick[:, 1::2] != 0)
    upward = jax.random.randint(key_list[6], (DEVICES, PAIR_DEV), 0, 2) * 2 - 1
    other_group = group_of[:, None] + upward
    other_group = jnp.where(other_group < 0, group_of[:, None] + 1, jnp.where(other_group >= N_GROUP, group_of[:, None] - 1, other_group))
    rim_pick = jax.random.randint(key_list[7], (DEVICES, PAIR_DEV), 0, RIM_VES)
    ghost_id = (other_group * N_MEMBER + member_of[:, None]) * VES_DEV + rim_pick
    first_ids = inside_id[:, 0::2]
    second_ids = jnp.where(ghost_flag, ghost_id, inside_id[:, 1::2])
    live_flag = jnp.arange(PAIR_DEV)[None, :] < live_count[:, None]
    first_ids = jnp.where(live_flag, first_ids, -1)
    second_ids = jnp.where(live_flag, second_ids, -1)
    return jnp.stack([first_ids, second_ids], axis=-1).reshape(PAIRS, 2).astype(jnp.int32)


def setup_inputs(seed: int = 0) -> dict:
    arg_keys = jax.random.split(jax.random.key(seed), 4)
    coefficients = draw_coefficients(jax.random.fold_in(arg_keys[3], 71), 0)
    pair_list = draw_pair_list(jax.random.fold_in(arg_keys[3], 71), 0)
    pair_offset = draw_pair_offset(jax.random.fold_in(arg_keys[3], 71), 0)
    return {"coefficients": coefficients, "pair_list": pair_list, "pair_offset": pair_offset}


def contact_width(up_order):
    return (0.7 * math.pi / (up_order + 1)) ** 2

def legendre_table(order_max, cosine, sine_theta):
    legendre = {}
    diagonal = jnp.ones_like(cosine) * math.sqrt(1.0 / (4.0 * math.pi))
    for azimuth in range(order_max + 1):
        if azimuth > 0:
            diagonal = -math.sqrt((2.0 * azimuth + 1.0) / (2.0 * azimuth)) * sine_theta * diagonal
        legendre[azimuth, azimuth] = diagonal
        if azimuth < order_max:
            legendre[azimuth + 1, azimuth] = math.sqrt(2.0 * azimuth + 3.0) * cosine * diagonal
        for degree in range(azimuth + 2, order_max + 1):
            factor_one = math.sqrt((4.0 * degree * degree - 1.0) / (degree * degree - azimuth * azimuth))
            factor_two = math.sqrt(((degree - 1.0) ** 2 - azimuth * azimuth) / (4.0 * (degree - 1.0) ** 2 - 1.0))
            legendre[degree, azimuth] = factor_one * (cosine * legendre[degree - 1, azimuth] - factor_two * legendre[degree - 2, azimuth])
    return legendre

def basis_table(order_max, up_order):
    lat_count = up_order + 1
    lon_count = 2 * up_order
    polar_angle = (jnp.arange(lat_count, dtype=jnp.float32) + 0.5) * (math.pi / lat_count)
    longitude = jnp.arange(lon_count, dtype=jnp.float32) * (2.0 * math.pi / lon_count)
    cosine = jnp.cos(polar_angle)
    sine_theta = jnp.sin(polar_angle)
    legendre = legendre_table(order_max, cosine, sine_theta)
    ones_row = jnp.ones_like(longitude)
    basis_rows = []
    for degree in range(order_max + 1):
        for azimuth in range(-degree, degree + 1):
            if azimuth == 0:
                beside_all = ones_row
            elif azimuth > 0:
                beside_all = math.sqrt(2.0) * jnp.cos(azimuth * longitude)
            else:
                beside_all = math.sqrt(2.0) * jnp.sin(-azimuth * longitude)
            basis_rows.append((legendre[degree, abs(azimuth)][:, None] * beside_all[None, :]).reshape(-1))
    harmonics = jnp.stack(basis_rows)
    weights = (sine_theta[:, None] * ones_row[None, :]).reshape(-1) * (math.pi / lat_count) * (2.0 * math.pi / lon_count)
    return (harmonics, weights)

def upsample(coef_block, harmonics):
    vesicle_count = coef_block.shape[0]
    surface = jnp.dot(coef_block.reshape(vesicle_count * 3, -1), harmonics, precision=lax.Precision.HIGHEST, preferred_element_type=jnp.float32)
    return surface.reshape(vesicle_count, 3, -1)

def project(point_force, harmonics, weights):
    vesicle_count = point_force.shape[0]
    weighted = (point_force * weights[None, None, :]).reshape(vesicle_count * 3, -1)
    result = jnp.dot(weighted, harmonics.T, precision=lax.Precision.HIGHEST, preferred_element_type=jnp.float32)
    return result.reshape(vesicle_count, 3, -1)

def pair_forces(near_side, far_side, width):
    factor = 1.0 / (near_side.shape[1] * width * width)
    delta_x = near_side[0][:, None] - far_side[0][None, :]
    delta_y = near_side[1][:, None] - far_side[1][None, :]
    delta_z = near_side[2][:, None] - far_side[2][None, :]
    dist_sq = delta_x * delta_x + delta_y * delta_y + delta_z * delta_z
    kernel = 1.0 / (1.0 + dist_sq / width)
    kernel = kernel * kernel
    on_near = jnp.stack([lax.optimization_barrier(jnp.sum(kernel * delta_x, axis=1)), lax.optimization_barrier(jnp.sum(kernel * delta_y, axis=1)), lax.optimization_barrier(jnp.sum(kernel * delta_z, axis=1))]) * factor
    on_far = -jnp.stack([lax.optimization_barrier(jnp.sum(kernel * delta_x, axis=0)), lax.optimization_barrier(jnp.sum(kernel * delta_y, axis=0)), lax.optimization_barrier(jnp.sum(kernel * delta_z, axis=0))]) * factor
    return (on_near, on_far)

def reference(coefficients, pair_list, pair_offset):
    harmonics, weights = basis_table(ORDER, UPORDER)
    width = contact_width(UPORDER)
    surfaces = upsample(coefficients, harmonics)

    def add_pair(point_force, pair_data):
        pair_ids, offset_row = pair_data
        first_id = jnp.maximum(pair_ids[0], 0).astype(jnp.int32)
        second_id = jnp.maximum(pair_ids[1], 0).astype(jnp.int32)
        near_side = lax.dynamic_index_in_dim(surfaces, first_id, 0, keepdims=False) + offset_row[:, None]
        far_side = lax.dynamic_index_in_dim(surfaces, second_id, 0, keepdims=False)

        def live_branch(unused):
            return pair_forces(near_side, far_side, width)

        def dead_branch(unused):
            return (jnp.zeros_like(near_side), jnp.zeros_like(near_side))
        on_near, on_far = lax.cond(pair_ids[0] >= 0, live_branch, dead_branch, 0)
        point_force = point_force.at[first_id].add(on_near)
        point_force = point_force.at[second_id].add(on_far)
        return (point_force, None)
    point_force, unused = lax.scan(add_pair, jnp.zeros_like(surfaces), (pair_list, pair_offset))
    return project(point_force, harmonics, weights)
```

```python
import math

import jax
import jax.numpy as jnp
import numpy as np
from jax import lax
from jax.experimental import pallas as pl
from jax.experimental.pallas import tpu as pltpu
from jax.sharding import PartitionSpec as P

ORDER = 16
UPORDER = 32
RIM_VES = 4
LATS = UPORDER + 1
LONS = 2 * UPORDER
POINTS = LATS * LONS
PADDED = -(-POINTS // 128) * 128
WIDTH = (0.7 * math.pi / (UPORDER + 1)) ** 2
FACTOR = 1.0 / (POINTS * WIDTH * WIDTH)
STRIP = 256
HIGHEST = lax.Precision.HIGHEST


def legendre_table(order_max, cosine, sine_theta):
    legendre = {}
    diagonal = np.ones_like(cosine) * math.sqrt(1.0 / (4.0 * math.pi))
    for azimuth in range(order_max + 1):
        if azimuth > 0:
            diagonal = -math.sqrt((2.0 * azimuth + 1.0) / (2.0 * azimuth)) * sine_theta * diagonal
        legendre[azimuth, azimuth] = diagonal
        if azimuth < order_max:
            legendre[azimuth + 1, azimuth] = math.sqrt(2.0 * azimuth + 3.0) * cosine * diagonal
        for degree in range(azimuth + 2, order_max + 1):
            factor_one = math.sqrt(
                (4.0 * degree * degree - 1.0) / (degree * degree - azimuth * azimuth)
            )
            factor_two = math.sqrt(
                ((degree - 1.0) ** 2 - azimuth * azimuth) / (4.0 * (degree - 1.0) ** 2 - 1.0)
            )
            legendre[degree, azimuth] = factor_one * (
                cosine * legendre[degree - 1, azimuth] - factor_two * legendre[degree - 2, azimuth]
            )
    return legendre


def point_order():
    order = []
    for lat_block in range(LATS // 8):
        for lon_block in range(LONS // 16):
            for lat in range(8):
                for lon in range(16):
                    order.append((lat_block * 8 + lat) * LONS + lon_block * 16 + lon)
    order.extend(range((LATS // 8) * 8 * LONS, POINTS))
    return np.array(order)


def basis_table():
    polar_angle = (np.arange(LATS) + 0.5) * (math.pi / LATS)
    longitude = np.arange(LONS) * (2.0 * math.pi / LONS)
    sine_theta = np.sin(polar_angle)
    legendre = legendre_table(ORDER, np.cos(polar_angle), sine_theta)
    rows = []
    for degree in range(ORDER + 1):
        for azimuth in range(-degree, degree + 1):
            if azimuth == 0:
                beside_all = np.ones_like(longitude)
            elif azimuth > 0:
                beside_all = math.sqrt(2.0) * np.cos(azimuth * longitude)
            else:
                beside_all = math.sqrt(2.0) * np.sin(-azimuth * longitude)
            rows.append((legendre[degree, abs(azimuth)][:, None] * beside_all[None, :]).reshape(-1))
    weights = np.repeat(sine_theta, LONS) * (math.pi / LATS) * (2.0 * math.pi / LONS)
    order = point_order()
    harmonics = np.zeros((len(rows), PADDED))
    harmonics[:, :POINTS] = np.stack(rows)[:, order]
    weighted = np.zeros_like(harmonics)
    weighted[:, :POINTS] = harmonics[:, :POINTS] * weights[order]
    return harmonics.astype(np.float32), np.ascontiguousarray(weighted.T).astype(np.float32)


def split(value):
    high = value.astype(jnp.bfloat16).astype(jnp.float32)
    rest = value - high
    mid = rest.astype(jnp.bfloat16).astype(jnp.float32)
    low = (rest - mid).astype(jnp.bfloat16).astype(jnp.float32)
    return high, mid, low


def stack_rows(*parts):
    rows = sum(part.shape[0] for part in parts)
    zeros = jnp.zeros((-rows % 16, parts[0].shape[1]), jnp.float32)
    return jnp.concatenate([*parts, zeros], axis=0)


def pair_kernel(live_ref, ends_ref, out_ref, near_scratch, far_scratch, sums_scratch):
    pair = pl.program_id(0)

    @pl.when(pair >= live_ref[0])
    def dead():
        out_ref[...] = jnp.zeros_like(out_ref)

    @pl.when(pair < live_ref[0])
    def live():
        near = ends_ref[0, 0]
        far = ends_ref[0, 1]
        lane = lax.broadcasted_iota(jnp.int32, (1, PADDED), 1)
        valid = lane < POINTS
        one = jnp.ones((1, PADDED), jnp.float32)
        n_high, n_mid, n_low = split(near)
        f_high, f_mid, f_low = split(far * (-2.0 / WIDTH))
        n_sq = split(1.0 + jnp.sum(near * near, axis=0, keepdims=True) * (1.0 / WIDTH))
        f_sq = split(jnp.sum(far * far, axis=0, keepdims=True) * (1.0 / WIDTH))
        left = stack_rows(
            n_high, n_high, n_mid, n_mid, n_high, n_low, *n_sq, one, one, one
        )
        right = stack_rows(
            f_high, f_mid, f_high, f_mid, f_low, f_high, one, one, one, *f_sq
        )
        near_scratch[...] = jnp.transpose(left).astype(jnp.bfloat16)
        far_scratch[...] = right.astype(jnp.bfloat16)
        near_rows = stack_rows(n_high, n_mid, n_low, one).astype(jnp.bfloat16)
        g_high, g_mid, g_low = split(far)
        far_rows = jnp.where(valid, stack_rows(g_high, g_mid, g_low, one), 0.0).astype(jnp.bfloat16)
        sums_scratch[1] = jnp.zeros((16, PADDED), jnp.float32)
        sums_scratch[0] = jnp.zeros((16, PADDED), jnp.float32)
        rows_scratch_near = near_rows
        rows_scratch_far = far_rows

        for start in range(0, POINTS, STRIP):
            size = min(STRIP, POINTS - start)
            left_strip = near_scratch[start : start + size, :]
            near_strip = rows_scratch_near[:, start : start + size]
            near_sum = jnp.zeros((16, size), jnp.float32)
            for column in range(0, PADDED, 256):
                span = min(256, PADDED - column)
                reach = jnp.dot(
                    left_strip,
                    far_scratch[:, column : column + span],
                    preferred_element_type=jnp.float32,
                )
                inverse = pl.reciprocal(reach, approx=True)
                kernel = inverse * inverse
                high = kernel.astype(jnp.bfloat16)
                low = (kernel - high.astype(jnp.float32)).astype(jnp.bfloat16)
                sums_scratch[1, :, column : column + span] += jnp.dot(
                    near_strip, high, preferred_element_type=jnp.float32
                ) + jnp.dot(near_strip, low, preferred_element_type=jnp.float32)
                far_part = rows_scratch_far[:, column : column + span]
                across = (((1,), (1,)), ((), ()))
                near_sum += lax.dot_general(
                    far_part, high, across, preferred_element_type=jnp.float32
                ) + lax.dot_general(far_part, low, across, preferred_element_type=jnp.float32)
            sums_scratch[0, :, start : start + size] = near_sum

        for side, here in ((0, near), (1, far)):
            sums = sums_scratch[side]
            others = sums[0:3] + sums[3:6] + sums[6:9]
            out_ref[0, side] = (here * sums[9:10] - others) * FACTOR


def all_pair_forces(live_count, ends):
    pair_count = ends.shape[0]
    block = (1, 2, 3, PADDED)
    depth = 32
    return pl.pallas_call(
        pair_kernel,
        grid_spec=pltpu.PrefetchScalarGridSpec(
            num_scalar_prefetch=1,
            grid=(pair_count,),
            in_specs=[pl.BlockSpec(block, lambda p, live: (p, 0, 0, 0))],
            out_specs=pl.BlockSpec(block, lambda p, live: (p, 0, 0, 0)),
            scratch_shapes=[
                pltpu.VMEM((PADDED, depth), jnp.bfloat16),
                pltpu.VMEM((depth, PADDED), jnp.bfloat16),
                pltpu.VMEM((2, 16, PADDED), jnp.float32),
            ],
        ),
        out_shape=jax.ShapeDtypeStruct(ends.shape, jnp.float32),
        compiler_params=pltpu.CompilerParams(vmem_limit_bytes=48 * 1024 * 1024),
    )(live_count, ends)


def per_device(coefficients, pair_list, pair_offset):
    members = lax.axis_size("member")
    groups = lax.axis_size("group")
    group_here = lax.axis_index("group")
    vesicle_count = coefficients.shape[0]
    pair_count = pair_list.shape[0]
    coef_count = coefficients.shape[2]
    slot_cap = max(2, (2 * pair_count + members - 1) // members)
    total_slots = members * slot_cap
    harmonics, weighted = basis_table()
    upward = [(i, i + 1) for i in range(groups - 1)]
    downward = [(i + 1, i) for i in range(groups - 1)]

    end_ids = pair_list.reshape(-1)
    end_live = end_ids >= 0
    safe_ids = jnp.maximum(end_ids, 0)
    owner_device = safe_ids // vesicle_count
    owner_group = owner_device // members
    owner_member = owner_device % members
    owner_slot = safe_ids % vesicle_count
    inside = end_live & (owner_group == group_here)
    outside = end_live & (owner_group != group_here)

    flat = coefficients.reshape(vesicle_count, -1)
    gathered = lax.all_gather(flat, "member", tiled=True)
    below = lax.ppermute(flat[:RIM_VES], "group", upward)
    above = lax.ppermute(flat[:RIM_VES], "group", downward)
    table = jnp.concatenate([gathered, below, above], axis=0)
    rim_row = jnp.where(owner_group > group_here, RIM_VES, 0) + jnp.minimum(owner_slot, RIM_VES - 1)
    table_row = jnp.where(
        inside, owner_member * vesicle_count + owner_slot, members * vesicle_count + rim_row
    )
    pick = (table_row[:, None] == jnp.arange(table.shape[0])[None, :]).astype(jnp.float32)
    end_coef = jnp.dot(pick, table, precision=HIGHEST)
    ends = jnp.dot(
        end_coef.reshape(2 * pair_count * 3, coef_count), harmonics, precision=HIGHEST
    ).reshape(pair_count, 2, 3, PADDED)
    halves = jnp.stack([0.5 * pair_offset, -0.5 * pair_offset], axis=1)
    ends = ends + halves[..., None]
    live_count = jnp.sum(end_live.astype(jnp.int32)).reshape(1) // 2
    forces = all_pair_forces(live_count, ends)
    projected = jnp.dot(
        forces.reshape(2 * pair_count * 3, PADDED), weighted, precision=HIGHEST
    ).reshape(2 * pair_count, 3 * coef_count)

    rim_pick = ((jnp.arange(2 * RIM_VES)[:, None] == rim_row[None, :]) & outside[None, :]).astype(
        jnp.float32
    )
    rim_force = jnp.dot(rim_pick, projected, precision=HIGHEST)
    from_above = lax.ppermute(rim_force[:RIM_VES], "group", downward)
    from_below = lax.ppermute(rim_force[RIM_VES:], "group", upward)

    member_hits = (
        (owner_member[:, None] == jnp.arange(members)[None, :]) & inside[:, None]
    ).astype(jnp.int32)
    earlier = jnp.sum((jnp.cumsum(member_hits, axis=0) - member_hits) * member_hits, axis=1)
    end_slot = owner_member * slot_cap + earlier
    slot_pick = ((jnp.arange(total_slots)[:, None] == end_slot[None, :]) & inside[None, :]).astype(
        jnp.float32
    )
    tagged = jnp.concatenate([projected, owner_slot[:, None].astype(jnp.float32)], axis=1)
    outgoing = jnp.dot(slot_pick, tagged, precision=HIGHEST)
    incoming = lax.all_to_all(
        outgoing.reshape(members, slot_cap, -1), "member", split_axis=0, concat_axis=0, tiled=True
    ).reshape(total_slots, -1)
    tags = incoming[:, -1]
    selector = (
        tags[None, :] == jnp.arange(vesicle_count, dtype=jnp.float32)[:, None]
    ).astype(jnp.float32)
    total = jnp.dot(selector, incoming[:, :-1], precision=HIGHEST)
    total = total.at[:RIM_VES].add(from_above + from_below)
    return total.reshape(coefficients.shape)


def solution(mesh):
    return jax.shard_map(
        per_device,
        mesh=mesh,
        in_specs=(
            P(("group", "member"), None, None),
            P(("group", "member"), None),
            P(("group", "member"), None),
        ),
        out_specs=P(("group", "member"), None, None),
        check_vma=False,
    )
```

```python
import math

import jax
import jax.numpy as jnp
import numpy as np
from jax import lax
from jax.experimental import pallas as pl
from jax.experimental.pallas import tpu as pltpu
from jax.sharding import PartitionSpec as P

ORDER = 16
UPORDER = 32
RIM_VES = 4
LATS = UPORDER + 1
LONS = 2 * UPORDER
POINTS = LATS * LONS
PADDED = -(-POINTS // 128) * 128
WIDTH = (0.7 * math.pi / (UPORDER + 1)) ** 2
FACTOR = 1.0 / (POINTS * WIDTH * WIDTH)
ROWS = POINTS // 3
CHUNKS = ((0, 512), (512, 512), (1024, 512), (1536, PADDED - 1536))
BEYOND = 1e30
HIGHEST = lax.Precision.HIGHEST


def legendre_table(order_max, cosine, sine_theta):
    legendre = {}
    diagonal = np.ones_like(cosine) * math.sqrt(1.0 / (4.0 * math.pi))
    for azimuth in range(order_max + 1):
        if azimuth > 0:
            diagonal = -math.sqrt((2.0 * azimuth + 1.0) / (2.0 * azimuth)) * sine_theta * diagonal
        legendre[azimuth, azimuth] = diagonal
        if azimuth < order_max:
            legendre[azimuth + 1, azimuth] = math.sqrt(2.0 * azimuth + 3.0) * cosine * diagonal
        for degree in range(azimuth + 2, order_max + 1):
            factor_one = math.sqrt(
                (4.0 * degree * degree - 1.0) / (degree * degree - azimuth * azimuth)
            )
            factor_two = math.sqrt(
                ((degree - 1.0) ** 2 - azimuth * azimuth) / (4.0 * (degree - 1.0) ** 2 - 1.0)
            )
            legendre[degree, azimuth] = factor_one * (
                cosine * legendre[degree - 1, azimuth] - factor_two * legendre[degree - 2, azimuth]
            )
    return legendre


def point_order():
    order = []
    for lat_block in range(LATS // 8):
        for lon_block in range(LONS // 16):
            for lat in range(8):
                for lon in range(16):
                    order.append((lat_block * 8 + lat) * LONS + lon_block * 16 + lon)
    order.extend(range((LATS // 8) * 8 * LONS, POINTS))
    return np.array(order)


def basis_table():
    polar_angle = (np.arange(LATS) + 0.5) * (math.pi / LATS)
    longitude = np.arange(LONS) * (2.0 * math.pi / LONS)
    sine_theta = np.sin(polar_angle)
    legendre = legendre_table(ORDER, np.cos(polar_angle), sine_theta)
    rows = []
    for degree in range(ORDER + 1):
        for azimuth in range(-degree, degree + 1):
            if azimuth == 0:
                beside_all = np.ones_like(longitude)
            elif azimuth > 0:
                beside_all = math.sqrt(2.0) * np.cos(azimuth * longitude)
            else:
                beside_all = math.sqrt(2.0) * np.sin(-azimuth * longitude)
            rows.append((legendre[degree, abs(azimuth)][:, None] * beside_all[None, :]).reshape(-1))
    weights = np.repeat(sine_theta, LONS) * (math.pi / LATS) * (2.0 * math.pi / LONS)
    order = point_order()
    harmonics = np.zeros((len(rows), PADDED))
    harmonics[:, :POINTS] = np.stack(rows)[:, order]
    weighted = np.zeros_like(harmonics)
    weighted[:, :POINTS] = harmonics[:, :POINTS] * weights[order]
    return harmonics.astype(np.float32), np.ascontiguousarray(weighted.T).astype(np.float32)


def split(value):
    high = value.astype(jnp.bfloat16).astype(jnp.float32)
    rest = value - high
    mid = rest.astype(jnp.bfloat16).astype(jnp.float32)
    low = (rest - mid).astype(jnp.bfloat16).astype(jnp.float32)
    return high, mid, low


def pair_kernel(live_ref, ends_ref, out_ref, left_ref, right_ref, near_ref, far_ref, sums_ref):
    pair = pl.program_id(0)

    @pl.when(pair >= live_ref[0])
    def dead():
        out_ref[...] = jnp.zeros_like(out_ref)

    @pl.when(pair < live_ref[0])
    def live():
        near = ends_ref[0, 0]
        far = ends_ref[0, 1]
        lane = lax.broadcasted_iota(jnp.int32, (1, PADDED), 1)
        valid = lane < POINTS
        one = jnp.ones((1, PADDED), jnp.float32)
        zeros = jnp.zeros((8, PADDED), jnp.float32)
        n_high, n_mid, n_low = split(near)
        f_high, f_mid, f_low = split(far * (-2.0 / WIDTH))
        n_sq = split(1.0 + jnp.sum(near * near, axis=0, keepdims=True) * (1.0 / WIDTH))
        f_sq = jnp.sum(far * far, axis=0, keepdims=True) * (1.0 / WIDTH)
        f_sq = split(jnp.where(valid, f_sq, BEYOND))
        left = [n_high, n_high, n_mid, n_mid, n_high, n_low, *n_sq, one, one, one, near, zeros[:5]]
        right = [f_high, f_mid, f_high, f_mid, f_low, f_high, one, one, one, *f_sq, zeros]
        turned = jnp.transpose(jnp.concatenate(left, axis=0))
        left_ref[...] = turned.astype(jnp.bfloat16)
        right_ref[...] = jnp.concatenate(right, axis=0).astype(jnp.bfloat16)
        for axis in range(3):
            near_ref[axis] = jnp.broadcast_to(turned[:, 24 + axis : 25 + axis], (PADDED, 128))
            far_ref[axis] = jnp.broadcast_to(far[axis : axis + 1], (8, PADDED))

        for start, size in CHUNKS:
            lanes = [slice(start + k, start + k + 128) for k in range(0, size, 128)]
            count = len(lanes)

            def block(index, totals, start=start, size=size, lanes=lanes, count=count):
                first = pl.multiple_of(index * ROWS, ROWS)
                reach = jnp.dot(
                    left_ref[pl.ds(first, ROWS), :],
                    right_ref[:, start : start + size],
                    preferred_element_type=jnp.float32,
                )
                totals = list(totals)
                for group in range(ROWS // 8):
                    rows = pl.ds(first + group * 8, 8)
                    here = [near_ref[axis, rows, :] for axis in range(3)]
                    partial = [None] * 3
                    for k in range(count):
                        inverse = pl.reciprocal(
                            reach[group * 8 : group * 8 + 8, k * 128 : k * 128 + 128], approx=True
                        )
                        kernel = inverse * inverse
                        for axis in range(3):
                            term = kernel * (here[axis] - far_ref[axis, :, lanes[k]])
                            slot = axis * count + k
                            totals[slot] = totals[slot] + term
                            partial[axis] = term if k == 0 else partial[axis] + term
                    for axis in range(3):
                        if start:
                            partial[axis] = partial[axis] + sums_ref[axis, rows, :]
                        sums_ref[axis, rows, :] = partial[axis]
                return tuple(totals)

            zero = jnp.zeros((8, 128), jnp.float32)
            totals = lax.fori_loop(0, POINTS // ROWS, block, (zero,) * (3 * count))
            for axis in range(3):
                for k in range(count):
                    out_ref[0, 1, axis : axis + 1, lanes[k]] = (
                        jnp.sum(totals[axis * count + k], axis=0, keepdims=True) * -FACTOR
                    )

        for axis in range(3):
            total = jnp.sum(jnp.transpose(sums_ref[axis]), axis=0, keepdims=True)
            out_ref[0, 0, axis : axis + 1, :] = jnp.where(valid, total * FACTOR, 0.0)


def all_pair_forces(live_count, ends):
    pair_count = ends.shape[0]
    block = (1, 2, 3, PADDED)
    depth = 32
    return pl.pallas_call(
        pair_kernel,
        grid_spec=pltpu.PrefetchScalarGridSpec(
            num_scalar_prefetch=1,
            grid=(pair_count,),
            in_specs=[pl.BlockSpec(block, lambda p, live: (p, 0, 0, 0))],
            out_specs=pl.BlockSpec(block, lambda p, live: (p, 0, 0, 0)),
            scratch_shapes=[
                pltpu.VMEM((PADDED, depth), jnp.bfloat16),
                pltpu.VMEM((depth, PADDED), jnp.bfloat16),
                pltpu.VMEM((3, PADDED, 128), jnp.float32),
                pltpu.VMEM((3, 8, PADDED), jnp.float32),
                pltpu.VMEM((3, PADDED, 128), jnp.float32),
            ],
        ),
        out_shape=jax.ShapeDtypeStruct(ends.shape, jnp.float32),
        compiler_params=pltpu.CompilerParams(vmem_limit_bytes=48 * 1024 * 1024),
    )(live_count, ends)


def per_device(coefficients, pair_list, pair_offset):
    members = lax.axis_size("member")
    groups = lax.axis_size("group")
    group_here = lax.axis_index("group")
    vesicle_count = coefficients.shape[0]
    pair_count = pair_list.shape[0]
    coef_count = coefficients.shape[2]
    slot_cap = max(2, (2 * pair_count + members - 1) // members)
    total_slots = members * slot_cap
    harmonics, weighted = basis_table()
    upward = [(i, i + 1) for i in range(groups - 1)]
    downward = [(i + 1, i) for i in range(groups - 1)]

    end_ids = pair_list.reshape(-1)
    end_live = end_ids >= 0
    safe_ids = jnp.maximum(end_ids, 0)
    owner_device = safe_ids // vesicle_count
    owner_group = owner_device // members
    owner_member = owner_device % members
    owner_slot = safe_ids % vesicle_count
    inside = end_live & (owner_group == group_here)
    outside = end_live & (owner_group != group_here)

    flat = coefficients.reshape(vesicle_count, -1)
    gathered = lax.all_gather(flat, "member", tiled=True)
    below = lax.ppermute(flat[:RIM_VES], "group", upward)
    above = lax.ppermute(flat[:RIM_VES], "group", downward)
    table = jnp.concatenate([gathered, below, above], axis=0)
    rim_row = jnp.where(owner_group > group_here, RIM_VES, 0) + jnp.minimum(owner_slot, RIM_VES - 1)
    table_row = jnp.where(
        inside, owner_member * vesicle_count + owner_slot, members * vesicle_count + rim_row
    )
    pick = (table_row[:, None] == jnp.arange(table.shape[0])[None, :]).astype(jnp.float32)
    end_coef = jnp.dot(pick, table, precision=HIGHEST)
    ends = jnp.dot(
        end_coef.reshape(2 * pair_count * 3, coef_count), harmonics, precision=HIGHEST
    ).reshape(pair_count, 2, 3, PADDED)
    halves = jnp.stack([0.5 * pair_offset, -0.5 * pair_offset], axis=1)
    ends = ends + halves[..., None]
    live_count = jnp.sum(end_live.astype(jnp.int32)).reshape(1) // 2
    forces = all_pair_forces(live_count, ends)
    projected = jnp.dot(
        forces.reshape(2 * pair_count * 3, PADDED), weighted, precision=HIGHEST
    ).reshape(2 * pair_count, 3 * coef_count)

    rim_pick = ((jnp.arange(2 * RIM_VES)[:, None] == rim_row[None, :]) & outside[None, :]).astype(
        jnp.float32
    )
    rim_force = jnp.dot(rim_pick, projected, precision=HIGHEST)
    from_above = lax.ppermute(rim_force[:RIM_VES], "group", downward)
    from_below = lax.ppermute(rim_force[RIM_VES:], "group", upward)

    member_hits = (
        (owner_member[:, None] == jnp.arange(members)[None, :]) & inside[:, None]
    ).astype(jnp.int32)
    earlier = jnp.sum((jnp.cumsum(member_hits, axis=0) - member_hits) * member_hits, axis=1)
    end_slot = owner_member * slot_cap + earlier
    slot_pick = ((jnp.arange(total_slots)[:, None] == end_slot[None, :]) & inside[None, :]).astype(
        jnp.float32
    )
    tagged = jnp.concatenate([projected, owner_slot[:, None].astype(jnp.float32)], axis=1)
    outgoing = jnp.dot(slot_pick, tagged, precision=HIGHEST)
    incoming = lax.all_to_all(
        outgoing.reshape(members, slot_cap, -1), "member", split_axis=0, concat_axis=0, tiled=True
    ).reshape(total_slots, -1)
    tags = incoming[:, -1]
    selector = (
        tags[None, :] == jnp.arange(vesicle_count, dtype=jnp.float32)[:, None]
    ).astype(jnp.float32)
    total = jnp.dot(selector, incoming[:, :-1], precision=HIGHEST)
    total = total.at[:RIM_VES].add(from_above + from_below)
    return total.reshape(coefficients.shape)


def solution(mesh):
    return jax.shard_map(
        per_device,
        mesh=mesh,
        in_specs=(
            P(("group", "member"), None, None),
            P(("group", "member"), None),
            P(("group", "member"), None),
        ),
        out_specs=P(("group", "member"), None, None),
        check_vma=False,
    )
```
